32 devices in a mesh: ta: 4 (over z), tp: 8 (over y, x, core).
Axes of the slice: x: 2, y: 2, z: 4, core: 2. Of those that a mesh axis runs over, the one named last changes fastest.
Arguments:
- lesser_history: bfloat16 [8, 8, 256, 512], P('ta', 'tp'), as said below
- greater_history: bfloat16 [8, 8, 256, 512], P('ta', 'tp'), as said below
- newest_lesser_row: bfloat16 [8, 256, 512], P('tp'), may hold values from -4 to 4
- newest_greater_row: bfloat16 [8, 256, 512], P('tp'), may hold values from -4 to 4
- propagator: bfloat16 [256, 512], replicated
Outputs:
- row_less_out: bfloat16 [8, 256, 512], P('tp')
- row_great_out: bfloat16 [8, 256, 512], P('tp')
The draws below stay inside these ranges and needn't reach their ends.
Inputs may be any that keep to these rules, and one draw needn't show every extreme that they name: lesser_history[t', t] is minus the conjugate transpose of lesser_history[t, t'] for all stored times: its real part is the negated transpose, its imaginary part the transpose. greater_history[t', t] is minus the conjugate transpose of greater_history[t, t'] for all stored times.
All inputs are finite; a program needn't handle non-finite values.
Results may differ from the reference program's by a relative error of at most 0.012.
Values may be sent and summed in bfloat16 or wider, within the bound.
A program may use at most 64 MiB of HBM per device.

```python
import jax
import jax.numpy as jnp
from jax import lax

NO = 256
STEPS = 2
NT = 8


def skew_hermitian(base):
    width = base.shape[-2]
    real = base[..., :width]
    imag = base[..., width:]
    real_t = jnp.transpose(real, (1, 0, 3, 2))
    imag_t = jnp.transpose(imag, (1, 0, 3, 2))
    return jnp.concatenate([real - real_t, imag + imag_t], -1).astype(jnp.bfloat16)


def draw_lesser_history(key, part):
    key = jax.random.fold_in(key, 11)
    scale = (2.0 * NT * NO) ** (-0.5)
    base = jax.random.normal(key, (NT, NT, NO, 2 * NO), jnp.float32) * scale
    return skew_hermitian(base)


def draw_greater_history(key, part):
    key = jax.random.fold_in(key, 12)
    scale = (2.0 * NT * NO) ** (-0.5)
    base = jax.random.normal(key, (NT, NT, NO, 2 * NO), jnp.float32) * scale
    return skew_hermitian(base)


def draw_propagator(key, part):
    key = jax.random.fold_in(key, 5)
    noise = jax.random.normal(key, (NO, 2 * NO), jnp.float32) * (0.3 * (2.0 * NO) ** (-0.5))
    ids = jnp.arange(NO, dtype=jnp.int32)
    unit = (ids[:, None] == ids[None, :]).astype(jnp.float32)
    return jnp.concatenate([unit + noise[:, :NO], noise[:, NO:]], -1).astype(jnp.bfloat16)


def levels(own_key, dims, cuts, low, top_value):
    level = 1.0
    for position, parts in cuts:
        steps = jax.random.uniform(jax.random.fold_in(jax.random.fold_in(own_key, 6), position), (parts,), jnp.float32, low / len(cuts), top_value / len(cuts))
        level = level * jnp.repeat(jnp.exp(steps), dims[position] // parts).reshape((-1,) + (1,) * (len(dims) - 1 - position))
    return level


def centred(rng, shape, scale, limit, cuts=(), kind=jnp.bfloat16):
    values = scale * jax.random.normal(rng, shape, jnp.float32)
    if cuts:
        values = values * levels(rng, shape, cuts, -0.22, 0.18)
    return jnp.clip(values, -limit, limit).astype(kind)


def setup_inputs(seed: int = 0) -> dict:
    splits = jax.random.split(jax.random.key(seed), 6)
    return {
        "lesser_history": draw_lesser_history(jax.random.fold_in(splits[5], 71), 0),
        "greater_history": draw_greater_history(jax.random.fold_in(splits[5], 71), 0),
        "newest_lesser_row": centred(splits[2], (NT, NO, 2 * NO), 0.7, 4.0, ((0, 8),)),
        "newest_greater_row": centred(splits[3], (NT, NO, 2 * NO), 0.7, 4.0, ((0, 8),)),
        "propagator": draw_propagator(jax.random.fold_in(splits[5], 71), 0),
    }


time_increment = 0.3


def split_complex_parts(tiles):
    width = tiles.shape[-2]
    return tiles[..., :width], tiles[..., width:]


def self_energy(row_l, row_g):
    less_real, less_imag = split_complex_parts(row_l.astype(jnp.float32))
    great_real, great_imag = split_complex_parts(row_g.astype(jnp.float32))
    lsq_real = less_real * less_real - less_imag * less_imag
    lsq_imag = 2.0 * less_real * less_imag
    gsq_real = great_real * great_real - great_imag * great_imag
    gsq_imag = 2.0 * great_real * great_imag
    sigma_lesser = jnp.concatenate([-(lsq_real * great_real + lsq_imag * great_imag), -(lsq_imag * great_real - lsq_real * great_imag)], -1)
    sigma_greater = jnp.concatenate([-(gsq_real * less_real + gsq_imag * less_imag), -(gsq_imag * less_real - gsq_real * less_imag)], -1)
    sigma_retarded = sigma_greater - sigma_lesser
    return sigma_lesser.astype(jnp.bfloat16), sigma_greater.astype(jnp.bfloat16), sigma_retarded.astype(jnp.bfloat16)


def summed_product(left, right):
    left_real, left_imag = split_complex_parts(left)
    right_real, right_imag = split_complex_parts(right)
    real = jnp.einsum("tik,tkj->ij", left_real, right_real) - jnp.einsum("tik,tkj->ij", left_imag, right_imag)
    imag = jnp.einsum("tik,tkj->ij", left_real, right_imag) + jnp.einsum("tik,tkj->ij", left_imag, right_real)
    return jnp.concatenate([real, imag], -1)


def advance_rows(propagator, row_entry, collision_term):
    row_real_part, row_imaginary = split_complex_parts(row_entry.astype(jnp.float32))
    collision_real, collision_imaginary = split_complex_parts(collision_term)
    mixed_term = jnp.concatenate([row_real_part + time_increment * collision_imaginary, row_imaginary - time_increment * collision_real], -1)
    mixed_term = lax.optimization_barrier(mixed_term.astype(jnp.bfloat16)).astype(jnp.float32)
    mix_real, mix_imag = split_complex_parts(mixed_term)
    prop_real, prop_imag = split_complex_parts(propagator.astype(jnp.float32))
    real = jnp.einsum("ik,tkj->tij", prop_real, mix_real) - jnp.einsum("ik,tkj->tij", prop_imag, mix_imag)
    imag = jnp.einsum("ik,tkj->tij", prop_real, mix_imag) + jnp.einsum("ik,tkj->tij", prop_imag, mix_real)
    return jnp.concatenate([real, imag], -1).astype(jnp.bfloat16)


def reference(lesser_history, greater_history, newest_lesser_row, newest_greater_row, propagator):
    total = lesser_history.shape[0]
    diff = (greater_history.astype(jnp.float32) - lesser_history.astype(jnp.float32)).astype(jnp.bfloat16)
    time_points = jnp.arange(total, dtype=jnp.int32)
    for step in range(STEPS):
        sigma_lesser, sigma_greater, sigma_retarded = self_energy(newest_lesser_row, newest_greater_row)
        lesser_factor = sigma_lesser.astype(jnp.float32)
        greater_factor = sigma_greater.astype(jnp.float32)
        retarded_factor = sigma_retarded.astype(jnp.float32)

        def column_entry(index):
            history_lesser = lax.dynamic_index_in_dim(lesser_history, index, 1, keepdims=False).astype(jnp.float32)
            history_greater = lax.dynamic_index_in_dim(greater_history, index, 1, keepdims=False).astype(jnp.float32)
            hist_diff = lax.dynamic_index_in_dim(diff, index, 1, keepdims=False).astype(jnp.float32)
            earlier = (time_points < index)[:, None, None]
            masked_entries = jnp.where(earlier, hist_diff, jnp.zeros_like(hist_diff))
            collision_lesser = summed_product(retarded_factor, history_lesser) - summed_product(lesser_factor, masked_entries)
            collision_greater = summed_product(retarded_factor, history_greater) - summed_product(greater_factor, masked_entries)
            return collision_lesser, collision_greater

        collision_lesser_sum, collision_greater_sum = lax.map(column_entry, time_points)
        newest_lesser_row, newest_greater_row = advance_rows(propagator, newest_lesser_row, collision_lesser_sum), advance_rows(propagator, newest_greater_row, collision_greater_sum)
    return newest_lesser_row, newest_greater_row
```

```python
import jax
import jax.numpy as jnp
from jax import lax
from jax.experimental import pallas as pl
from jax.experimental.pallas import tpu as pltpu
from jax.sharding import PartitionSpec as P

time_increment = 0.3
MESH = pl.DeviceIdType.MESH
f32 = jnp.float32
bf16 = jnp.bfloat16


def self_energy(row_l, row_g):
    w = row_l.shape[-1] // 2
    lr, li = row_l[:, :w].astype(f32), row_l[:, w:].astype(f32)
    gr, gi = row_g[:, :w].astype(f32), row_g[:, w:].astype(f32)
    lsr, lsi = lr * lr - li * li, 2.0 * lr * li
    gsr, gsi = gr * gr - gi * gi, 2.0 * gr * gi
    less = (-(lsr * gr + lsi * gi), -(lsi * gr - lsr * gi))
    great = (-(gsr * lr + gsi * li), -(gsi * lr - gsr * li))
    return less, great


def factors(row_l, row_g, below):
    (lr, li), (gr, gi) = self_energy(row_l, row_g)
    on_l = (jnp.where(below, gr, gr - lr), jnp.where(below, gi, gi - li))
    on_g = (jnp.where(below, -lr, gr - lr), jnp.where(below, -li, gi - li))
    return on_l, on_g


def complex_square(tile):
    w = tile.shape[0]
    re, im = tile[:, :w], tile[:, w:]
    return jnp.concatenate(
        [jnp.concatenate([re, im], 1), jnp.concatenate([-im, re], 1)], 0
    )


def rotate(coll):
    w = coll.shape[-1] // 2
    return jnp.concatenate(
        [time_increment * coll[:, w:], -time_increment * coll[:, :w]], 1
    )


def kernel(
    na,
    nt,
    less_ref,
    great_ref,
    rowl_ref,
    rowg_ref,
    prop_ref,
    outl_ref,
    outg_ref,
    part,
    sib_in,
    pre,
    rs_in,
    gath,
    zpart,
    zin,
    zg,
    stored_l,
    stored_g,
    sib_s,
    sib_r,
    rs_s,
    rs_r,
    ag_s,
    ag_r,
    fw_s,
    fw_r,
    zr_s,
    zr_r,
    za_s,
    za_r,
):
    nq = nt // 2
    w = prop_ref.shape[0]
    br = w // nq
    a = lax.axis_index("ta")
    c = lax.axis_index("tp")
    q = c // 2
    h = c - 2 * q
    other = 1 - h
    sib = 2 * q + other

    barrier = pltpu.get_barrier_semaphore()
    pl.semaphore_signal(barrier, inc=1, device_id={"tp": sib}, device_id_type=MESH)
    for k in range(1, nq):
        to = 2 * lax.rem(q + k, nq) + h
        pl.semaphore_signal(barrier, inc=1, device_id={"tp": to}, device_id_type=MESH)
    for k in range(1, na):
        to = lax.rem(a + k, na)
        pl.semaphore_signal(barrier, inc=1, device_id={"ta": to}, device_id_type=MESH)

    def remote(src, dst, ss, rs, **to):
        return pltpu.make_async_remote_copy(
            src_ref=src, dst_ref=dst, send_sem=ss, recv_sem=rs, device_id=to, device_id_type=MESH
        )

    row_l, row_g = rowl_ref[0], rowg_ref[0]
    prop = prop_ref[...]
    for i in range(2):
        r = 2 * a + i
        below = c < r
        on_l, on_g = factors(row_l, row_g, below)
        prods = []
        for (re, im), stored in ((on_l, less_ref), (on_g, great_ref)):
            re, im = re.astype(bf16), im.astype(bf16)
            lhs = jnp.concatenate(
                [jnp.concatenate([-im, re], 1), jnp.concatenate([re, im], 1)], 0
            )
            res = lax.dot_general(
                lhs, stored[i, 0], (((1,), (1,)), ((), ())), preferred_element_type=f32
            )
            prods.append(jnp.concatenate([res[:w], res[w:]], 1) * time_increment)
        both = jnp.where(below, 1.0, 0.0).astype(f32)
        mine = jnp.where(c == r, 1.0, 0.0).astype(f32)
        for kind in range(2):
            row = (row_l, row_g)[kind].astype(f32)
            mixed = prods[kind] + both * prods[1 - kind] + mine * row
            new = jnp.dot(prop, complex_square(mixed.astype(bf16)), preferred_element_type=f32)
            new = new.astype(bf16)
            for g in range(nq):
                part[g, i, kind] = new[g * br : (g + 1) * br]

    pl.semaphore_wait(barrier, nq + na - 1)

    order = [k % nq for k in range(1, nq + 1)]
    sends = []
    for k in order:
        g = lax.rem(q + k, nq)
        cp = remote(part.at[g, other], sib_in.at[k], sib_s.at[k], sib_r.at[k], tp=sib)
        cp.start()
        sends.append(cp)

    for i in range(2):
        stored_l[i] = complex_square(less_ref[i, 0])
        stored_g[i] = complex_square(great_ref[i, 0])

    rs = {}
    for k in order:
        g = lax.rem(q + k, nq)
        remote(part.at[g, other], sib_in.at[k], sib_s.at[k], sib_r.at[k], tp=sib).wait_recv()
        total = part[g, h].astype(f32) + sib_in[k].astype(f32)
        if k:
            pre[k] = total.astype(bf16)
            cp = remote(pre.at[k], rs_in.at[k], rs_s.at[k], rs_r.at[k], tp=2 * g + h)
            cp.start()
            rs[k] = cp
            sends.append(cp)
    for k in range(1, nq):
        rs[k].wait_recv()
        total = total + rs_in[k].astype(f32)
    gath[q, h] = total.astype(bf16)

    ag = {}
    for k in range(1, nq):
        g = lax.rem(q + k, nq)
        cp = remote(gath.at[q, h], gath.at[q, h], ag_s.at[k], ag_r.at[k], tp=2 * g + h)
        cp.start()
        ag[k] = cp
        sends.append(cp)

    def forward(g, k, half):
        return remote(gath.at[g, half], gath.at[g, half], fw_s.at[k], fw_r.at[k], tp=sib)

    cp = forward(q, 0, h)
    cp.start()
    sends.append(cp)

    for k in range(nq):
        g = lax.rem(q - k + nq, nq)
        if k:
            remote(gath.at[g, h], gath.at[g, h], ag_s.at[k], ag_r.at[k], tp=sib).wait_recv()
            cp = forward(g, k, h)
            cp.start()
            sends.append(cp)
        forward(g, k, other).wait_recv()

        colls = [jnp.zeros((br, 2 * w), f32), jnp.zeros((br, 2 * w), f32)]
        for i in range(2):
            below = 2 * a + i < c
            both = jnp.where(below, 1.0, 0.0).astype(f32)
            on_l, on_g = factors(gath[g, i, 0], gath[g, i, 1], below)
            prods = []
            for (re, im), stored in ((on_l, stored_l), (on_g, stored_g)):
                lhs = jnp.concatenate([re, im], 1).astype(bf16)
                prods.append(jnp.dot(lhs, stored[i], preferred_element_type=f32))
            for kind in range(2):
                colls[kind] = colls[kind] + prods[kind] + both * prods[1 - kind]
        mine = jnp.where(q == a, 1.0, 0.0).astype(f32)
        for kind in range(2):
            mixed = rotate(colls[kind]) + mine * gath[g, h, kind].astype(f32)
            zpart[g, kind] = mixed.astype(bf16)

        @pl.when(g != a)
        def _():
            remote(zpart.at[g], zin.at[a], zr_s.at[g], zr_r.at[a], ta=g).start()

    total = zpart[a].astype(f32)
    for j in range(1, na):
        b = lax.rem(a + j, na)
        remote(zpart.at[b], zin.at[b], zr_s.at[b], zr_r.at[b], ta=b).wait_recv()
        total = total + zin[b].astype(f32)
    zg[a] = total.astype(bf16)

    for j in range(1, na):
        b = lax.rem(a + j, na)
        cp = remote(zg.at[a], zg.at[a], za_s.at[j], za_r.at[j], ta=b)
        cp.start()
        sends.append(cp)
    for j in range(1, na):
        b = lax.rem(a - j + na, na)
        remote(zg.at[b], zg.at[b], za_s.at[j], za_r.at[j], ta=b).wait_recv()
    for kind, out in ((0, outl_ref), (1, outg_ref)):
        mixed = jnp.concatenate([zg[b, kind] for b in range(na)], 0)
        out[0] = jnp.dot(prop, complex_square(mixed), preferred_element_type=f32).astype(bf16)

    for cp in sends:
        cp.wait_send()
    for j in range(1, na):
        b = lax.rem(a + j, na)
        remote(zpart.at[b], zin.at[b], zr_s.at[b], zr_r.at[b], ta=b).wait_send()


def solution(mesh):
    na, nt = mesh.shape["ta"], mesh.shape["tp"]
    nq = nt // 2

    def local(less, great, rowl, rowg, prop):
        w = prop.shape[0]
        br = w // nq
        chunk = (2, br, 2 * w)
        dma = pltpu.SemaphoreType.DMA
        out = jax.ShapeDtypeStruct(rowl.shape, rowl.dtype)
        return pl.pallas_call(
            lambda *refs: kernel(na, nt, *refs),
            out_shape=(out, out),
            in_specs=[pl.BlockSpec(memory_space=pltpu.VMEM)] * 5,
            out_specs=(pl.BlockSpec(memory_space=pltpu.VMEM),) * 2,
            scratch_shapes=[
                pltpu.VMEM((nq, 2) + chunk, bf16),
                pltpu.VMEM((nq,) + chunk, bf16),
                pltpu.VMEM((nq,) + chunk, bf16),
                pltpu.VMEM((nq,) + chunk, bf16),
                pltpu.VMEM((nq, 2) + chunk, bf16),
                pltpu.VMEM((na,) + chunk, bf16),
                pltpu.VMEM((na,) + chunk, bf16),
                pltpu.VMEM((na,) + chunk, bf16),
                pltpu.VMEM((2, 2 * w, 2 * w), bf16),
                pltpu.VMEM((2, 2 * w, 2 * w), bf16),
            ]
            + [dma((nq,))] * 8
            + [dma((na,))] * 4,
            compiler_params=pltpu.CompilerParams(
                collective_id=0, has_side_effects=True, vmem_limit_bytes=48 * 1024 * 1024
            ),
            name="advance",
        )(less, great, rowl, rowg, prop)

    placed = (
        P("ta", "tp", None, None),
        P("ta", "tp", None, None),
        P("tp", None, None),
        P("tp", None, None),
        P(),
    )
    return jax.shard_map(
        local,
        mesh=mesh,
        in_specs=placed,
        out_specs=(P("tp", None, None), P("tp", None, None)),
        check_vma=False,
    )
```

```python
import jax
import jax.numpy as jnp
from jax import lax
from jax.experimental import pallas as pl
from jax.experimental.pallas import tpu as pltpu
from jax.sharding import PartitionSpec as P

time_increment = 0.3
MESH = pl.DeviceIdType.MESH
f32 = jnp.float32
bf16 = jnp.bfloat16


def self_energy(row_l, row_g):
    w = row_l.shape[-1] // 2
    lr, li = row_l[:, :w].astype(f32), row_l[:, w:].astype(f32)
    gr, gi = row_g[:, :w].astype(f32), row_g[:, w:].astype(f32)
    lsr, lsi = lr * lr - li * li, 2.0 * lr * li
    gsr, gsi = gr * gr - gi * gi, 2.0 * gr * gi
    less = (-(lsr * gr + lsi * gi), -(lsi * gr - lsr * gi))
    great = (-(gsr * lr + gsi * li), -(gsi * lr - gsr * li))
    return less, great


def factors(row_l, row_g, below):
    (lr, li), (gr, gi) = self_energy(row_l, row_g)
    on_l = (jnp.where(below, gr, gr - lr), jnp.where(below, gi, gi - li))
    on_g = (jnp.where(below, -lr, gr - lr), jnp.where(below, -li, gi - li))
    return on_l, on_g


def complex_square(tile):
    w = tile.shape[0]
    re, im = tile[:, :w], tile[:, w:]
    return jnp.concatenate(
        [jnp.concatenate([re, im], 1), jnp.concatenate([-im, re], 1)], 0
    )


def rotate(coll):
    w = coll.shape[-1] // 2
    return jnp.concatenate(
        [time_increment * coll[:, w:], -time_increment * coll[:, :w]], 1
    )


def kernel(
    na,
    nt,
    nu,
    less_hbm,
    great_hbm,
    rowl_hbm,
    rowg_hbm,
    prop_hbm,
    outl_ref,
    outg_ref,
    less_ref,
    great_ref,
    rows_ref,
    prop_ref,
    part,
    sib_in,
    pre,
    rs_in,
    gath,
    zpart,
    zsib,
    zpre,
    zin,
    zg,
    stored_l,
    stored_g,
    load,
    sib_s,
    sib_r,
    rs_s,
    rs_r,
    ag_s,
    ag_r,
    fw_s,
    fw_r,
    zs_s,
    zs_r,
    zr_s,
    zr_r,
    za_s,
    za_r,
    zf_s,
    zf_r,
):
    nq = nt // 2
    npair = na // 2
    w = prop_ref.shape[0]
    wu = w // nu
    br = wu // nq
    a = lax.axis_index("ta")
    c = lax.axis_index("tp")
    q = c // 2
    h = c - 2 * q
    other = 1 - h
    sib = 2 * q + other
    pa = a // 2
    ha = a - 2 * pa
    zsibling = 2 * pa + 1 - ha

    def fetch(src, dst, n):
        return pltpu.make_async_copy(src, dst, load.at[n])

    loads = [
        fetch(rowl_hbm.at[0], rows_ref.at[0], 0),
        fetch(rowg_hbm.at[0], rows_ref.at[1], 1),
        fetch(less_hbm.at[other, 0], less_ref.at[other], 2),
        fetch(great_hbm.at[other, 0], great_ref.at[other], 3),
        fetch(prop_hbm, prop_ref, 4),
        fetch(less_hbm.at[h, 0], less_ref.at[h], 5),
        fetch(great_hbm.at[h, 0], great_ref.at[h], 6),
    ]
    for cp in loads:
        cp.start()

    barrier = pltpu.get_barrier_semaphore()
    pl.semaphore_signal(barrier, inc=1, device_id={"tp": sib}, device_id_type=MESH)
    for k in range(1, nq):
        to = 2 * lax.rem(q + k, nq) + h
        pl.semaphore_signal(barrier, inc=1, device_id={"tp": to}, device_id_type=MESH)
    pl.semaphore_signal(barrier, inc=1, device_id={"ta": zsibling}, device_id_type=MESH)
    for k in range(1, npair):
        to = 2 * lax.rem(pa + k, npair) + ha
        pl.semaphore_signal(barrier, inc=1, device_id={"ta": to}, device_id_type=MESH)

    def remote(src, dst, ss, rs, **to):
        return pltpu.make_async_remote_copy(
            src_ref=src, dst_ref=dst, send_sem=ss, recv_sem=rs, device_id=to, device_id_type=MESH
        )

    sends = []

    def launch(cp):
        cp.start()
        sends.append(cp)

    loads[0].wait()
    loads[1].wait()
    row_l, row_g = rows_ref[0], rows_ref[1]
    (lr, li), (gr, gi) = self_energy(row_l, row_g)

    def first(i):
        r = 2 * a + i
        below = c < r
        on_l = (jnp.where(below, gr, gr - lr), jnp.where(below, gi, gi - li))
        on_g = (jnp.where(below, -lr, gr - lr), jnp.where(below, -li, gi - li))
        prods = []
        for (re, im), stored in ((on_l, less_ref), (on_g, great_ref)):
            re, im = re.astype(bf16), im.astype(bf16)
            lhs = jnp.concatenate(
                [jnp.concatenate([-im, re], 1), jnp.concatenate([re, im], 1)], 0
            )
            res = lax.dot_general(
                lhs, stored[i], (((1,), (1,)), ((), ())), preferred_element_type=f32
            )
            prods.append(jnp.concatenate([res[:w], res[w:]], 1) * time_increment)
        both = jnp.where(below, 1.0, 0.0).astype(f32)
        mine = jnp.where(c == r, 1.0, 0.0).astype(f32)
        for kind in range(2):
            row = (row_l, row_g)[kind].astype(f32)
            mixed = prods[kind] + both * prods[1 - kind] + mine * row
            new = jnp.dot(
                prop_ref[...], complex_square(mixed.astype(bf16)), preferred_element_type=f32
            )
            new = new.astype(bf16)
            for u in range(nu):
                for g in range(nq):
                    at = u * wu + g * br
                    part[g, i, u, kind] = new[at : at + br]

    for n in (2, 3, 4):
        loads[n].wait()
    first(other)

    pl.semaphore_wait(barrier, nq + npair)

    order = [k % nq for k in range(1, nq + 1)]

    def to_sibling(k, u):
        g = lax.rem(q + k, nq)
        return remote(part.at[g, other, u], sib_in.at[k, u], sib_s.at[k, u], sib_r.at[k, u], tp=sib)

    for u in range(nu):
        for k in order:
            launch(to_sibling(k, u))
    loads[5].wait()
    loads[6].wait()
    first(h)

    def scatter(k, u):
        g = lax.rem(q + k, nq)
        return remote(pre.at[k, u], rs_in.at[k, u], rs_s.at[k, u], rs_r.at[k, u], tp=2 * g + h)

    kept = []
    for u in range(nu):
        for k in order:
            g = lax.rem(q + k, nq)
            to_sibling(k, u).wait_recv()
            total = part[g, h, u].astype(f32) + sib_in[k, u].astype(f32)
            if k:
                pre[k, u] = total.astype(bf16)
                launch(scatter(k, u))
            else:
                kept.append(total)

    for i in range(2):
        stored_l[i] = complex_square(less_ref[i])
        stored_g[i] = complex_square(great_ref[i])

    def gather(k, u):
        g = lax.rem(q + k, nq)
        return remote(gath.at[q, h, u], gath.at[q, h, u], ag_s.at[k, u], ag_r.at[k, u], tp=2 * g + h)

    def forward(k, u, half):
        g = lax.rem(q - k + nq, nq)
        return remote(gath.at[g, half, u], gath.at[g, half, u], fw_s.at[k, u], fw_r.at[k, u], tp=sib)

    for u in range(nu):
        total = kept[u]
        for k in range(1, nq):
            scatter(k, u).wait_recv()
            total = total + rs_in[k, u].astype(f32)
        gath[q, h, u] = total.astype(bf16)
        for k in range(1, nq):
            launch(gather(k, u))
        launch(forward(0, u, h))

    def z_sibling(pair, u):
        b = 2 * pair + 1 - ha
        return remote(zpart.at[b, u], zsib.at[pair, u], zs_s.at[pair, u], zs_r.at[pair, u], ta=zsibling)

    def second(k, u):
        g = lax.rem(q - k + nq, nq)
        forward(k, u, other).wait_recv()
        colls = [jnp.zeros((br, 2 * w), f32), jnp.zeros((br, 2 * w), f32)]
        for i in range(2):
            below = 2 * a + i < c
            both = jnp.where(below, 1.0, 0.0).astype(f32)
            on_l, on_g = factors(gath[g, i, u, 0], gath[g, i, u, 1], below)
            prods = []
            for (re, im), stored in ((on_l, stored_l), (on_g, stored_g)):
                lhs = jnp.concatenate([re, im], 1).astype(bf16)
                prods.append(jnp.dot(lhs, stored[i], preferred_element_type=f32))
            for kind in range(2):
                colls[kind] = colls[kind] + prods[kind] + both * prods[1 - kind]
        mine = jnp.where(q == a, 1.0, 0.0).astype(f32)
        for kind in range(2):
            mixed = rotate(colls[kind]) + mine * gath[g, h, u, kind].astype(f32)
            zpart[g, u, kind] = mixed.astype(bf16)
        pair = g // 2

        @pl.when(g - 2 * pair != ha)
        def _():
            z_sibling(pair, u).start()

    def z_scatter(k, u):
        b = 2 * lax.rem(pa + k, npair) + ha
        return remote(zpre.at[k, u], zin.at[k, u], zr_s.at[k, u], zr_r.at[k, u], ta=b)

    zkept = {}

    def z_pairs(u):
        for k in [k % npair for k in range(1, npair + 1)]:
            pair = lax.rem(pa + k, npair)
            z_sibling(pair, u).wait_recv()
            total = zpart[2 * pair + ha, u].astype(f32) + zsib[pair, u].astype(f32)
            if k:
                zpre[k, u] = total.astype(bf16)
                launch(z_scatter(k, u))
            else:
                zkept[u] = total

    def z_gather(k, u):
        b = 2 * lax.rem(pa + k, npair) + ha
        return remote(zg.at[a, u], zg.at[a, u], za_s.at[k, u], za_r.at[k, u], ta=b)

    def z_forward(k, u, half):
        b = 2 * lax.rem(pa - k + npair, npair) + half
        return remote(zg.at[b, u], zg.at[b, u], zf_s.at[k, u], zf_r.at[k, u], ta=zsibling)

    def z_finish(u):
        total = zkept[u]
        for k in range(1, npair):
            z_scatter(k, u).wait_recv()
            total = total + zin[k, u].astype(f32)
        zg[a, u] = total.astype(bf16)
        for k in range(1, npair):
            launch(z_gather(k, u))
        launch(z_forward(0, u, ha))

    for u in range(nu):
        for k in range(nq):
            if k:
                gather(k, u).wait_recv()
                launch(forward(k, u, h))
                second(k - 1, u)
            if u and k == nq // 2:
                z_pairs(u - 1)
        second(nq - 1, u)
        if u:
            z_finish(u - 1)
    z_pairs(nu - 1)
    z_finish(nu - 1)

    outs = [jnp.zeros((w, 2 * w), f32), jnp.zeros((w, 2 * w), f32)]
    for u in range(nu):
        for k in range(1, npair):
            z_gather(k, u).wait_recv()
            launch(z_forward(k, u, ha))
        for k in range(npair):
            z_forward(k, u, 1 - ha).wait_recv()
        at = u * wu
        left = jnp.concatenate(
            [prop_ref[:, at : at + wu], prop_ref[:, w + at : w + at + wu]], 1
        )
        for kind in range(2):
            mixed = jnp.concatenate([zg[b, u, kind] for b in range(na)], 0)
            re, im = mixed[:, :w], mixed[:, w:]
            right = jnp.concatenate(
                [jnp.concatenate([re, im], 1), jnp.concatenate([-im, re], 1)], 0
            )
            outs[kind] = outs[kind] + jnp.dot(left, right, preferred_element_type=f32)
    outl_ref[0] = outs[0].astype(bf16)
    outg_ref[0] = outs[1].astype(bf16)

    for cp in sends:
        cp.wait_send()
    for u in range(nu):
        for pair in range(npair):
            z_sibling(pair, u).wait_send()


def solution(mesh):
    na, nt = mesh.shape["ta"], mesh.shape["tp"]
    nq = nt // 2
    npair = na // 2

    def local(less, great, rowl, rowg, prop):
        w = prop.shape[0]
        nu = 2 if w // nq >= 32 else 1
        piece = (nu, 2, w // (nq * nu), 2 * w)
        dma = pltpu.SemaphoreType.DMA
        out = jax.ShapeDtypeStruct(rowl.shape, rowl.dtype)
        return pl.pallas_call(
            lambda *refs: kernel(na, nt, nu, *refs),
            out_shape=(out, out),
            in_specs=[pl.BlockSpec(memory_space=pltpu.HBM)] * 5,
            out_specs=(pl.BlockSpec(memory_space=pltpu.VMEM),) * 2,
            scratch_shapes=[
                pltpu.VMEM((2, w, 2 * w), bf16),
                pltpu.VMEM((2, w, 2 * w), bf16),
                pltpu.VMEM((2, w, 2 * w), bf16),
                pltpu.VMEM((w, 2 * w), bf16),
                pltpu.VMEM((nq, 2) + piece, bf16),
                pltpu.VMEM((nq,) + piece, bf16),
                pltpu.VMEM((nq,) + piece, bf16),
                pltpu.VMEM((nq,) + piece, bf16),
                pltpu.VMEM((nq, 2) + piece, bf16),
                pltpu.VMEM((na,) + piece, bf16),
                pltpu.VMEM((npair,) + piece, bf16),
                pltpu.VMEM((npair,) + piece, bf16),
                pltpu.VMEM((npair,) + piece, bf16),
                pltpu.VMEM((na,) + piece, bf16),
                pltpu.VMEM((2, 2 * w, 2 * w), bf16),
                pltpu.VMEM((2, 2 * w, 2 * w), bf16),
                dma((7,)),
            ]
            + [dma((nq, nu))] * 8
            + [dma((npair, nu))] * 8,
            compiler_params=pltpu.CompilerParams(
                collective_id=0, has_side_effects=True, vmem_limit_bytes=48 * 1024 * 1024
            ),
            name="advance",
        )(less, great, rowl, rowg, prop)

    placed = (
        P("ta", "tp", None, None),
        P("ta", "tp", None, None),
        P("tp", None, None),
        P("tp", None, None),
        P(),
    )
    return jax.shard_map(
        local,
        mesh=mesh,
        in_specs=placed,
        out_specs=(P("tp", None, None), P("tp", None, None)),
        check_vma=False,
    )
```

```python
import jax
import jax.numpy as jnp
from jax import lax
from jax.experimental import pallas as pl
from jax.experimental.pallas import tpu as pltpu
from jax.sharding import PartitionSpec as P

time_increment = 0.3
MESH = pl.DeviceIdType.MESH
f32 = jnp.float32
bf16 = jnp.bfloat16


def self_energy(row_l, row_g):
    w = row_l.shape[-1] // 2
    lr, li = row_l[:, :w].astype(f32), row_l[:, w:].astype(f32)
    gr, gi = row_g[:, :w].astype(f32), row_g[:, w:].astype(f32)
    lsr, lsi = lr * lr - li * li, 2.0 * lr * li
    gsr, gsi = gr * gr - gi * gi, 2.0 * gr * gi
    less = (-(lsr * gr + lsi * gi), -(lsi * gr - lsr * gi))
    great = (-(gsr * lr + gsi * li), -(gsi * lr - gsr * li))
    return less, great


def factors(row_l, row_g, below):
    (lr, li), (gr, gi) = self_energy(row_l, row_g)
    on_l = (jnp.where(below, gr, gr - lr), jnp.where(below, gi, gi - li))
    on_g = (jnp.where(below, -lr, gr - lr), jnp.where(below, -li, gi - li))
    return on_l, on_g


def complex_square(tile):
    w = tile.shape[0]
    re, im = tile[:, :w], tile[:, w:]
    return jnp.concatenate(
        [jnp.concatenate([re, im], 1), jnp.concatenate([-im, re], 1)], 0
    )


def rotate(coll):
    w = coll.shape[-1] // 2
    return jnp.concatenate(
        [time_increment * coll[:, w:], -time_increment * coll[:, :w]], 1
    )


def kernel(
    na,
    nt,
    nu,
    less_hbm,
    great_hbm,
    rowl_hbm,
    rowg_hbm,
    prop_hbm,
    outl_ref,
    outg_ref,
    less_ref,
    great_ref,
    rows_ref,
    prop_ref,
    part,
    sib_in,
    pre,
    rs_in,
    gath,
    zpart,
    zsib,
    zpre,
    zin,
    zg,
    stored_l,
    stored_g,
    load,
    sib_s,
    sib_r,
    rs_s,
    rs_r,
    ag_s,
    ag_r,
    fw_s,
    fw_r,
    zs_s,
    zs_r,
    zr_s,
    zr_r,
    za_s,
    za_r,
    zf_s,
    zf_r,
):
    nq = nt // 2
    npair = na // 2
    w = prop_ref.shape[0]
    wu = w // nu
    br = wu // nq
    a = lax.axis_index("ta")
    c = lax.axis_index("tp")
    q = c // 2
    h = c - 2 * q
    other = 1 - h
    sib = 2 * q + other
    pa = a // 2
    ha = a - 2 * pa
    zsibling = 2 * pa + 1 - ha

    def fetch(src, dst, n):
        return pltpu.make_async_copy(src, dst, load.at[n])

    loads = [
        fetch(rowl_hbm.at[0], rows_ref.at[0], 0),
        fetch(rowg_hbm.at[0], rows_ref.at[1], 1),
        fetch(less_hbm.at[other, 0], less_ref.at[other], 2),
        fetch(great_hbm.at[other, 0], great_ref.at[other], 3),
        fetch(prop_hbm, prop_ref, 4),
        fetch(less_hbm.at[h, 0], less_ref.at[h], 5),
        fetch(great_hbm.at[h, 0], great_ref.at[h], 6),
    ]
    for cp in loads:
        cp.start()

    barrier = pltpu.get_barrier_semaphore()
    pl.semaphore_signal(barrier, inc=1, device_id={"tp": sib}, device_id_type=MESH)
    for k in range(1, nq):
        to = 2 * lax.rem(q + k, nq) + h
        pl.semaphore_signal(barrier, inc=1, device_id={"tp": to}, device_id_type=MESH)
    pl.semaphore_signal(barrier, inc=1, device_id={"ta": zsibling}, device_id_type=MESH)
    for k in range(1, npair):
        to = 2 * lax.rem(pa + k, npair) + ha
        pl.semaphore_signal(barrier, inc=1, device_id={"ta": to}, device_id_type=MESH)

    def remote(src, dst, ss, rs, **to):
        return pltpu.make_async_remote_copy(
            src_ref=src, dst_ref=dst, send_sem=ss, recv_sem=rs, device_id=to, device_id_type=MESH
        )

    sends = []

    def launch(cp):
        cp.start()
        sends.append(cp)

    loads[0].wait()
    loads[1].wait()
    row_l, row_g = rows_ref[0], rows_ref[1]
    (lr, li), (gr, gi) = self_energy(row_l, row_g)

    def first(i):
        r = 2 * a + i
        below = c < r
        on_l = (jnp.where(below, gr, gr - lr), jnp.where(below, gi, gi - li))
        on_g = (jnp.where(below, -lr, gr - lr), jnp.where(below, -li, gi - li))
        prods = []
        for (re, im), stored in ((on_l, less_ref), (on_g, great_ref)):
            re, im = re.astype(bf16), im.astype(bf16)
            lhs = jnp.concatenate(
                [jnp.concatenate([-im, re], 1), jnp.concatenate([re, im], 1)], 0
            )
            res = lax.dot_general(
                lhs, stored[i], (((1,), (1,)), ((), ())), preferred_element_type=f32
            )
            prods.append(jnp.concatenate([res[:w], res[w:]], 1) * time_increment)
        both = jnp.where(below, 1.0, 0.0).astype(f32)
        mine = jnp.where(c == r, 1.0, 0.0).astype(f32)
        for kind in range(2):
            row = (row_l, row_g)[kind].astype(f32)
            mixed = prods[kind] + both * prods[1 - kind] + mine * row
            new = jnp.dot(
                prop_ref[...], complex_square(mixed.astype(bf16)), preferred_element_type=f32
            )
            new = new.astype(bf16)
            for u in range(nu):
                for g in range(nq):
                    at = u * wu + g * br
                    part[g, i, u, kind] = new[at : at + br]

    for n in (2, 3, 4):
        loads[n].wait()
    first(other)

    pl.semaphore_wait(barrier, nq + npair)

    order = [k % nq for k in range(1, nq + 1)]

    def to_sibling(k, u):
        g = lax.rem(q + k, nq)
        return remote(part.at[g, other, u], sib_in.at[k, u], sib_s.at[k, u], sib_r.at[k, u], tp=sib)

    for u in range(nu):
        for k in order:
            launch(to_sibling(k, u))
    loads[5].wait()
    loads[6].wait()
    first(h)

    for i in range(2):
        stored_l[i] = complex_square(less_ref[i])
        stored_g[i] = complex_square(great_ref[i])

    def scatter(k, u):
        g = lax.rem(q + k, nq)
        return remote(pre.at[k, u], rs_in.at[k, u], rs_s.at[k, u], rs_r.at[k, u], tp=2 * g + h)

    kept = []
    for u in range(nu):
        for k in order:
            g = lax.rem(q + k, nq)
            to_sibling(k, u).wait_recv()
            total = part[g, h, u].astype(f32) + sib_in[k, u].astype(f32)
            if k:
                pre[k, u] = total.astype(bf16)
                launch(scatter(k, u))
            else:
                kept.append(total)

    def gather(k, u):
        g = lax.rem(q + k, nq)
        return remote(gath.at[q, h, u], gath.at[q, h, u], ag_s.at[k, u], ag_r.at[k, u], tp=2 * g + h)

    def forward(k, u, half):
        g = lax.rem(q - k + nq, nq)
        return remote(gath.at[g, half, u], gath.at[g, half, u], fw_s.at[k, u], fw_r.at[k, u], tp=sib)

    for u in range(nu):
        total = kept[u]
        for k in range(1, nq):
            scatter(k, u).wait_recv()
            total = total + rs_in[k, u].astype(f32)
        gath[q, h, u] = total.astype(bf16)
        for k in range(1, nq):
            launch(gather(k, u))
        launch(forward(0, u, h))

    def z_sibling(pair, u):
        b = 2 * pair + 1 - ha
        return remote(zpart.at[b, u], zsib.at[pair, u], zs_s.at[pair, u], zs_r.at[pair, u], ta=zsibling)

    def second(k, u):
        g = lax.rem(q - k + nq, nq)
        forward(k, u, other).wait_recv()
        colls = [jnp.zeros((br, 2 * w), f32), jnp.zeros((br, 2 * w), f32)]
        for i in range(2):
            below = 2 * a + i < c
            both = jnp.where(below, 1.0, 0.0).astype(f32)
            on_l, on_g = factors(gath[g, i, u, 0], gath[g, i, u, 1], below)
            prods = []
            for (re, im), stored in ((on_l, stored_l), (on_g, stored_g)):
                lhs = jnp.concatenate([re, im], 1).astype(bf16)
                prods.append(jnp.dot(lhs, stored[i], preferred_element_type=f32))
            for kind in range(2):
                colls[kind] = colls[kind] + prods[kind] + both * prods[1 - kind]
        mine = jnp.where(q == a, 1.0, 0.0).astype(f32)
        for kind in range(2):
            mixed = rotate(colls[kind]) + mine * gath[g, h, u, kind].astype(f32)
            zpart[g, u, kind] = mixed.astype(bf16)
        pair = g // 2

        @pl.when(g - 2 * pair != ha)
        def _():
            z_sibling(pair, u).start()

    def z_scatter(k, u):
        b = 2 * lax.rem(pa + k, npair) + ha
        return remote(zpre.at[k, u], zin.at[k, u], zr_s.at[k, u], zr_r.at[k, u], ta=b)

    zkept = {}

    def z_pairs(u):
        for k in [k % npair for k in range(1, npair + 1)]:
            pair = lax.rem(pa + k, npair)
            z_sibling(pair, u).wait_recv()
            total = zpart[2 * pair + ha, u].astype(f32) + zsib[pair, u].astype(f32)
            if k:
                zpre[k, u] = total.astype(bf16)
                launch(z_scatter(k, u))
            else:
                zkept[u] = total

    def z_gather(k, u):
        b = 2 * lax.rem(pa + k, npair) + ha
        return remote(zg.at[a, u], zg.at[a, u], za_s.at[k, u], za_r.at[k, u], ta=b)

    def z_forward(k, u, half):
        b = 2 * lax.rem(pa - k + npair, npair) + half
        return remote(zg.at[b, u], zg.at[b, u], zf_s.at[k, u], zf_r.at[k, u], ta=zsibling)

    def z_finish(u):
        total = zkept[u]
        for k in range(1, npair):
            z_scatter(k, u).wait_recv()
            total = total + zin[k, u].astype(f32)
        zg[a, u] = total.astype(bf16)
        for k in range(1, npair):
            launch(z_gather(k, u))
        launch(z_forward(0, u, ha))

    for u in range(nu):
        for k in range(nq):
            if k:
                gather(k, u).wait_recv()
                launch(forward(k, u, h))
                second(k - 1, u)
            if u and k == nq // 2:
                z_pairs(u - 1)
        second(nq - 1, u)
        if u:
            z_finish(u - 1)
    z_pairs(nu - 1)
    z_finish(nu - 1)

    outs = [jnp.zeros((w, 2 * w), f32), jnp.zeros((w, 2 * w), f32)]
    for u in range(nu):
        for k in range(1, npair):
            z_gather(k, u).wait_recv()
            launch(z_forward(k, u, ha))
        for k in range(npair):
            z_forward(k, u, 1 - ha).wait_recv()
        at = u * wu
        left = jnp.concatenate(
            [prop_ref[:, at : at + wu], prop_ref[:, w + at : w + at + wu]], 1
        )
        for kind in range(2):
            mixed = jnp.concatenate([zg[b, u, kind] for b in range(na)], 0)
            re, im = mixed[:, :w], mixed[:, w:]
            right = jnp.concatenate(
                [jnp.concatenate([re, im], 1), jnp.concatenate([-im, re], 1)], 0
            )
            outs[kind] = outs[kind] + jnp.dot(left, right, preferred_element_type=f32)
    outl_ref[0] = outs[0].astype(bf16)
    outg_ref[0] = outs[1].astype(bf16)

    for cp in sends:
        cp.wait_send()
    for u in range(nu):
        for pair in range(npair):
            z_sibling(pair, u).wait_send()


def solution(mesh):
    na, nt = mesh.shape["ta"], mesh.shape["tp"]
    nq = nt // 2
    npair = na // 2

    def local(less, great, rowl, rowg, prop):
        w = prop.shape[0]
        nu = 2 if w // nq >= 32 else 1
        piece = (nu, 2, w // (nq * nu), 2 * w)
        dma = pltpu.SemaphoreType.DMA
        out = jax.ShapeDtypeStruct(rowl.shape, rowl.dtype)
        return pl.pallas_call(
            lambda *refs: kernel(na, nt, nu, *refs),
            out_shape=(out, out),
            in_specs=[pl.BlockSpec(memory_space=pltpu.HBM)] * 5,
            out_specs=(pl.BlockSpec(memory_space=pltpu.VMEM),) * 2,
            scratch_shapes=[
                pltpu.VMEM((2, w, 2 * w), bf16),
                pltpu.VMEM((2, w, 2 * w), bf16),
                pltpu.VMEM((2, w, 2 * w), bf16),
                pltpu.VMEM((w, 2 * w), bf16),
                pltpu.VMEM((nq, 2) + piece, bf16),
                pltpu.VMEM((nq,) + piece, bf16),
                pltpu.VMEM((nq,) + piece, bf16),
                pltpu.VMEM((nq,) + piece, bf16),
                pltpu.VMEM((nq, 2) + piece, bf16),
                pltpu.VMEM((na,) + piece, bf16),
                pltpu.VMEM((npair,) + piece, bf16),
                pltpu.VMEM((npair,) + piece, bf16),
                pltpu.VMEM((npair,) + piece, bf16),
                pltpu.VMEM((na,) + piece, bf16),
                pltpu.VMEM((2, 2 * w, 2 * w), bf16),
                pltpu.VMEM((2, 2 * w, 2 * w), bf16),
                dma((7,)),
            ]
            + [dma((nq, nu))] * 8
            + [dma((npair, nu))] * 8,
            compiler_params=pltpu.CompilerParams(
                collective_id=0, has_side_effects=True, vmem_limit_bytes=63 * 1024 * 1024 + 512 * 1024
            ),
            name="advance",
        )(less, great, rowl, rowg, prop)

    placed = (
        P("ta", "tp", None, None),
        P("ta", "tp", None, None),
        P("tp", None, None),
        P("tp", None, None),
        P(),
    )
    return jax.shard_map(
        local,
        mesh=mesh,
        in_specs=placed,
        out_specs=(P("tp", None, None), P("tp", None, None)),
        check_vma=False,
    )
```

```python
import jax
import jax.numpy as jnp
from jax import lax
from jax.experimental import pallas as pl
from jax.experimental.pallas import tpu as pltpu
from jax.sharding import PartitionSpec as P

time_increment = 0.3
MESH = pl.DeviceIdType.MESH
f32 = jnp.float32
bf16 = jnp.bfloat16


def self_energy(row_l, row_g):
    w = row_l.shape[-1] // 2
    lr, li = row_l[:, :w].astype(f32), row_l[:, w:].astype(f32)
    gr, gi = row_g[:, :w].astype(f32), row_g[:, w:].astype(f32)
    lsr, lsi = lr * lr - li * li, 2.0 * lr * li
    gsr, gsi = gr * gr - gi * gi, 2.0 * gr * gi
    less = (-(lsr * gr + lsi * gi), -(lsi * gr - lsr * gi))
    great = (-(gsr * lr + gsi * li), -(gsi * lr - gsr * li))
    return less, great


def factors(row_l, row_g, below):
    (lr, li), (gr, gi) = self_energy(row_l, row_g)
    on_l = (jnp.where(below, gr, gr - lr), jnp.where(below, gi, gi - li))
    on_g = (jnp.where(below, -lr, gr - lr), jnp.where(below, -li, gi - li))
    return on_l, on_g


def complex_square(tile):
    w = tile.shape[0]
    re, im = tile[:, :w], tile[:, w:]
    return jnp.concatenate(
        [jnp.concatenate([re, im], 1), jnp.concatenate([-im, re], 1)], 0
    )


def rotate(coll):
    w = coll.shape[-1] // 2
    return jnp.concatenate(
        [time_increment * coll[:, w:], -time_increment * coll[:, :w]], 1
    )


def kernel(
    na,
    nt,
    nu,
    less_hbm,
    great_hbm,
    rowl_hbm,
    rowg_hbm,
    prop_hbm,
    outl_ref,
    outg_ref,
    less_ref,
    great_ref,
    rows_ref,
    prop_ref,
    part,
    sib_in,
    pre,
    rs_in,
    gath,
    zpart,
    zsib,
    zpre,
    zin,
    zg,
    stored_l,
    stored_g,
    load,
    sib_s,
    sib_r,
    rs_s,
    rs_r,
    ag_s,
    ag_r,
    fw_s,
    fw_r,
    zs_s,
    zs_r,
    zr_s,
    zr_r,
    za_s,
    za_r,
    zf_s,
    zf_r,
):
    nq = nt // 2
    npair = na // 2
    w = prop_ref.shape[0]
    wu = w // nu
    br = wu // nq
    a = lax.axis_index("ta")
    c = lax.axis_index("tp")
    q = c // 2
    h = c - 2 * q
    other = 1 - h
    sib = 2 * q + other
    pa = a // 2
    ha = a - 2 * pa
    zsibling = 2 * pa + 1 - ha

    def fetch(src, dst, n):
        return pltpu.make_async_copy(src, dst, load.at[n])

    loads = [
        fetch(rowl_hbm.at[0], rows_ref.at[0], 0),
        fetch(rowg_hbm.at[0], rows_ref.at[1], 1),
        fetch(less_hbm.at[other, 0], less_ref.at[other], 2),
        fetch(great_hbm.at[other, 0], great_ref.at[other], 3),
        fetch(prop_hbm, prop_ref, 4),
        fetch(less_hbm.at[h, 0], less_ref.at[h], 5),
        fetch(great_hbm.at[h, 0], great_ref.at[h], 6),
    ]
    for cp in loads:
        cp.start()

    barrier = pltpu.get_barrier_semaphore()
    pl.semaphore_signal(barrier, inc=1, device_id={"tp": sib}, device_id_type=MESH)
    for k in range(1, nq):
        to = 2 * lax.rem(q + k, nq) + h
        pl.semaphore_signal(barrier, inc=1, device_id={"tp": to}, device_id_type=MESH)
    pl.semaphore_signal(barrier, inc=1, device_id={"ta": zsibling}, device_id_type=MESH)
    for k in range(1, npair):
        to = 2 * lax.rem(pa + k, npair) + ha
        pl.semaphore_signal(barrier, inc=1, device_id={"ta": to}, device_id_type=MESH)

    def remote(src, dst, ss, rs, **to):
        return pltpu.make_async_remote_copy(
            src_ref=src, dst_ref=dst, send_sem=ss, recv_sem=rs, device_id=to, device_id_type=MESH
        )

    sends = []

    def launch(cp):
        cp.start()
        sends.append(cp)

    loads[0].wait()
    loads[1].wait()
    row_l, row_g = rows_ref[0], rows_ref[1]
    (lr, li), (gr, gi) = self_energy(row_l, row_g)

    def first(i):
        r = 2 * a + i
        below = c < r
        on_l = (jnp.where(below, gr, gr - lr), jnp.where(below, gi, gi - li))
        on_g = (jnp.where(below, -lr, gr - lr), jnp.where(below, -li, gi - li))
        prods = []
        for (re, im), stored in ((on_l, less_ref), (on_g, great_ref)):
            re, im = re.astype(bf16), im.astype(bf16)
            lhs = jnp.concatenate(
                [jnp.concatenate([-im, re], 1), jnp.concatenate([re, im], 1)], 0
            )
            res = lax.dot_general(
                lhs, stored[i], (((1,), (1,)), ((), ())), preferred_element_type=f32
            )
            prods.append(jnp.concatenate([res[:w], res[w:]], 1) * time_increment)
        both = jnp.where(below, 1.0, 0.0).astype(f32)
        mine = jnp.where(c == r, 1.0, 0.0).astype(f32)
        for kind in range(2):
            row = (row_l, row_g)[kind].astype(f32)
            mixed = prods[kind] + both * prods[1 - kind] + mine * row
            new = jnp.dot(
                prop_ref[...], complex_square(mixed.astype(bf16)), preferred_element_type=f32
            )
            new = new.astype(bf16)
            for u in range(nu):
                for g in range(nq):
                    at = u * wu + g * br
                    part[g, i, u, kind] = new[at : at + br]

    for n in (2, 3, 4):
        loads[n].wait()
    first(other)

    pl.semaphore_wait(barrier, nq + npair)

    order = [k % nq for k in range(1, nq + 1)]

    def to_sibling(k, u):
        g = lax.rem(q + k, nq)
        return remote(part.at[g, other, u], sib_in.at[k, u], sib_s.at[k, u], sib_r.at[k, u], tp=sib)

    for u in range(nu):
        for k in order:
            launch(to_sibling(k, u))
    loads[5].wait()
    loads[6].wait()
    first(h)

    for i in range(2):
        stored_l[i] = complex_square(less_ref[i])
        stored_g[i] = complex_square(great_ref[i])

    def scatter(k, u):
        g = lax.rem(q + k, nq)
        return remote(pre.at[k, u], rs_in.at[k, u], rs_s.at[k, u], rs_r.at[k, u], tp=2 * g + h)

    kept = []
    for u in range(nu):
        for k in order:
            g = lax.rem(q + k, nq)
            to_sibling(k, u).wait_recv()
            total = part[g, h, u].astype(f32) + sib_in[k, u].astype(f32)
            if k:
                pre[k, u] = total.astype(bf16)
                launch(scatter(k, u))
            else:
                kept.append(total)

    def gather(k, u):
        g = lax.rem(q + k, nq)
        return remote(gath.at[q, h, u], gath.at[q, h, u], ag_s.at[k, u], ag_r.at[k, u], tp=2 * g + h)

    def forward(k, u, half):
        g = lax.rem(q - k + nq, nq)
        return remote(gath.at[g, half, u], gath.at[g, half, u], fw_s.at[k, u], fw_r.at[k, u], tp=sib)

    for u in range(nu):
        total = kept[u]
        for k in range(1, nq):
            scatter(k, u).wait_recv()
            total = total + rs_in[k, u].astype(f32)
        gath[q, h, u] = total.astype(bf16)
        for k in range(1, nq):
            launch(gather(k, u))
        launch(forward(0, u, h))

    def z_sibling(pair, u):
        b = 2 * pair + 1 - ha
        return remote(zpart.at[b, u], zsib.at[pair, u], zs_s.at[pair, u], zs_r.at[pair, u], ta=zsibling)

    def second(k, u):
        g = lax.rem(q - k + nq, nq)
        forward(k, u, other).wait_recv()
        colls = [jnp.zeros((br, 2 * w), f32), jnp.zeros((br, 2 * w), f32)]
        for i in range(2):
            below = 2 * a + i < c
            both = jnp.where(below, 1.0, 0.0).astype(f32)
            on_l, on_g = factors(gath[g, i, u, 0], gath[g, i, u, 1], below)
            prods = []
            for (re, im), stored in ((on_l, stored_l), (on_g, stored_g)):
                lhs = jnp.concatenate([re, im], 1).astype(bf16)
                prods.append(jnp.dot(lhs, stored[i], preferred_element_type=f32))
            for kind in range(2):
                colls[kind] = colls[kind] + prods[kind] + both * prods[1 - kind]
        mine = jnp.where(q == a, 1.0, 0.0).astype(f32)
        for kind in range(2):
            mixed = rotate(colls[kind]) + mine * gath[g, h, u, kind].astype(f32)
            zpart[g, u, kind] = mixed.astype(bf16)
        pair = g // 2

        @pl.when(g - 2 * pair != ha)
        def _():
            z_sibling(pair, u).start()

    def z_scatter(k, u):
        b = 2 * lax.rem(pa + k, npair) + ha
        return remote(zpre.at[k, u], zin.at[k, u], zr_s.at[k, u], zr_r.at[k, u], ta=b)

    zkept = {}

    def z_pairs(u):
        for k in [k % npair for k in range(1, npair + 1)]:
            pair = lax.rem(pa + k, npair)
            z_sibling(pair, u).wait_recv()
            total = zpart[2 * pair + ha, u].astype(f32) + zsib[pair, u].astype(f32)
            if k:
                zpre[k, u] = total.astype(bf16)
                launch(z_scatter(k, u))
            else:
                zkept[u] = total

    def z_gather(k, u):
        b = 2 * lax.rem(pa + k, npair) + ha
        return remote(zg.at[a, u], zg.at[a, u], za_s.at[k, u], za_r.at[k, u], ta=b)

    def z_forward(k, u, half):
        b = 2 * lax.rem(pa - k + npair, npair) + half
        return remote(zg.at[b, u], zg.at[b, u], zf_s.at[k, u], zf_r.at[k, u], ta=zsibling)

    def z_finish(u):
        total = zkept[u]
        for k in range(1, npair):
            z_scatter(k, u).wait_recv()
            total = total + zin[k, u].astype(f32)
        zg[a, u] = total.astype(bf16)
        for k in range(1, npair):
            launch(z_gather(k, u))
        launch(z_forward(0, u, ha))

    for u in range(nu):
        for k in range(nq):
            if k:
                gather(k, u).wait_recv()
                launch(forward(k, u, h))
                second(k - 1, u)
            if u and k == nq // 2:
                z_pairs(u - 1)
        second(nq - 1, u)
        if u:
            z_finish(u - 1)
    z_pairs(nu - 1)
    z_finish(nu - 1)

    outs = [jnp.zeros((w, 2 * w), f32), jnp.zeros((w, 2 * w), f32)]
    for u in range(nu):
        for k in range(1, npair):
            z_gather(k, u).wait_recv()
            launch(z_forward(k, u, ha))
    for u in range(nu):
        for k in range(npair):
            z_forward(k, u, 1 - ha).wait_recv()
        at = u * wu
        left = jnp.concatenate(
            [prop_ref[:, at : at + wu], prop_ref[:, w + at : w + at + wu]], 1
        )
        for kind in range(2):
            mixed = jnp.concatenate([zg[b, u, kind] for b in range(na)], 0)
            re, im = mixed[:, :w], mixed[:, w:]
            right = jnp.concatenate(
                [jnp.concatenate([re, im], 1), jnp.concatenate([-im, re], 1)], 0
            )
            outs[kind] = outs[kind] + jnp.dot(left, right, preferred_element_type=f32)
    outl_ref[0] = outs[0].astype(bf16)
    outg_ref[0] = outs[1].astype(bf16)

    for cp in sends:
        cp.wait_send()
    for u in range(nu):
        for pair in range(npair):
            z_sibling(pair, u).wait_send()


def solution(mesh):
    na, nt = mesh.shape["ta"], mesh.shape["tp"]
    nq = nt // 2
    npair = na // 2

    def local(less, great, rowl, rowg, prop):
        w = prop.shape[0]
        nu = 2 if w // nq >= 32 else 1
        piece = (nu, 2, w // (nq * nu), 2 * w)
        dma = pltpu.SemaphoreType.DMA
        out = jax.ShapeDtypeStruct(rowl.shape, rowl.dtype)
        return pl.pallas_call(
            lambda *refs: kernel(na, nt, nu, *refs),
            out_shape=(out, out),
            in_specs=[pl.BlockSpec(memory_space=pltpu.HBM)] * 5,
            out_specs=(pl.BlockSpec(memory_space=pltpu.VMEM),) * 2,
            scratch_shapes=[
                pltpu.VMEM((2, w, 2 * w), bf16),
                pltpu.VMEM((2, w, 2 * w), bf16),
                pltpu.VMEM((2, w, 2 * w), bf16),
                pltpu.VMEM((w, 2 * w), bf16),
                pltpu.VMEM((nq, 2) + piece, bf16),
                pltpu.VMEM((nq,) + piece, bf16),
                pltpu.VMEM((nq,) + piece, bf16),
                pltpu.VMEM((nq,) + piece, bf16),
                pltpu.VMEM((nq, 2) + piece, bf16),
                pltpu.VMEM((na,) + piece, bf16),
                pltpu.VMEM((npair,) + piece, bf16),
                pltpu.VMEM((npair,) + piece, bf16),
                pltpu.VMEM((npair,) + piece, bf16),
                pltpu.VMEM((na,) + piece, bf16),
                pltpu.VMEM((2, 2 * w, 2 * w), bf16),
                pltpu.VMEM((2, 2 * w, 2 * w), bf16),
                dma((7,)),
            ]
            + [dma((nq, nu))] * 8
            + [dma((npair, nu))] * 8,
            compiler_params=pltpu.CompilerParams(
                collective_id=0, has_side_effects=True, vmem_limit_bytes=63 * 1024 * 1024 + 512 * 1024
            ),
            name="advance",
        )(less, great, rowl, rowg, prop)

    placed = (
        P("ta", "tp", None, None),
        P("ta", "tp", None, None),
        P("tp", None, None),
        P("tp", None, None),
        P(),
    )
    return jax.shard_map(
        local,
        mesh=mesh,
        in_specs=placed,
        out_specs=(P("tp", None, None), P("tp", None, None)),
        check_vma=False,
    )
```
